32 devices in a mesh: src: 4 (over y, x), rcv: 4 (over z), seg: 2 (over core).
Axes of the slice: x: 2, y: 2, z: 4, core: 2. Of those that a mesh axis runs over, the one named last changes fastest.
Arguments:
- traces: bfloat16 [4, 512, 512], P('seg', 'src'), may hold values from -6 to 6
- fir_taps: bfloat16 [31], replicated, may hold values from -1 to 1
- pair_bins: int32 [512, 512], P('src', 'rcv'), may hold values from 0 to 1023, as said below
- bin_order: int32 [1024], replicated, may hold values from 0 to 1023, as said below
Outputs:
- owned_stacks: float32 [1024, 128], P(('src', 'rcv', 'seg'))
The draws below stay inside these ranges and needn't reach their ends.
Inputs may be any that keep to these rules, and one draw needn't show every extreme that they name: pair_bins[a, b] = floor((p_b - p_a) / 2) + 512 for channel positions p_c = 2 * c + e_c with e_c in 0 or 1, e of the first channel 0 and of the last 1; so pair_bins[a, b] is b - a + 511 or b - a + 512. bin_order holds every bin once; for every owner q the bins in rows q * 32 to (q + 1) * 32 - 1 are all congruent modulo 32.
All inputs are finite; a program needn't handle non-finite values.
Results may differ from the reference program's by a relative error of at most 0.0012.
Values may be sent and summed in bfloat16 or wider, within the bound.
No kernel may reach another device: no remote copies, remote signals or barrier semaphores. Data moves between devices by JAX's collectives and lax.ppermute only.
A program may use at most 64 MiB of HBM per device.

```python
import jax
import jax.numpy as jnp
from jax import lax

CH_BLOCK = 128
SAMPLES = 512
MAXLAG = 64
TAPS = 31
CHANNELS = 512
LAGS = 128
SEGS = 4
NBINS = 1024
OWNERS = 32
ROWS_OWNER = 32


def draw_pair_bins(key, part):
    channel = jnp.arange(CHANNELS, dtype=jnp.int32)
    jitter = jax.random.randint(jax.random.fold_in(key, 7), (CHANNELS,), 0, 2, dtype=jnp.int32)
    jitter = jnp.where(channel == 0, 0, jnp.where(channel == CHANNELS - 1, 1, jitter))
    position = 2 * channel + jitter
    return ((position[None, :] - position[:, None] + 2 * CHANNELS) // 2).astype(jnp.int32)


def draw_bin_order(key, part):
    residue = jax.random.permutation(jax.random.fold_in(key, 11), OWNERS).astype(jnp.int32)
    scores = jax.random.randint(jax.random.fold_in(key, 13), (OWNERS, ROWS_OWNER), 0, 1 << 20, dtype=jnp.int32)
    scores = scores * ROWS_OWNER + jnp.arange(ROWS_OWNER, dtype=jnp.int32)[None, :]
    within = jnp.argsort(scores, axis=1).astype(jnp.int32)
    return (within * OWNERS + residue[:, None]).reshape(-1).astype(jnp.int32)


def levels(stream_key, extent, shards, smallest, top_value):
    gain, own = 1.0, jax.random.fold_in(stream_key, 6)
    for dim, parts in shards:
        steps = jnp.exp(jax.random.uniform(jax.random.fold_in(own, dim), (parts,), jnp.float32, smallest / len(shards), top_value / len(shards)))
        gain = gain * jnp.repeat(steps, extent[dim] // parts).reshape([-1 if axis == dim else 1 for axis in range(len(extent))])
    return gain


def normal_values(key, extent, scale, reach, cuts=(), kind=jnp.bfloat16):
    result = jax.random.normal(key, extent, jnp.float32) * scale
    if len(cuts) > 0:
        result = levels(key, extent, cuts, -0.22, 0.18) * result
    return jnp.clip(result, min=-reach, max=reach).astype(kind)


def setup_inputs(seed: int = 0) -> dict:
    seeds = jax.random.split(jax.random.key(seed), 5)
    traces = normal_values(seeds[0], (SEGS, CHANNELS, SAMPLES), 1.0, 6.0, ((0, 2), (1, 4)))
    fir_taps = normal_values(seeds[1], (TAPS,), TAPS ** -0.5, 1.0)
    pair_bins = draw_pair_bins(jax.random.fold_in(seeds[4], 71), 0)
    bin_order = draw_bin_order(jax.random.fold_in(seeds[4], 71), 0)
    return {"traces": traces, "fir_taps": fir_taps, "pair_bins": pair_bins, "bin_order": bin_order}


def fir_matrix(fir_taps, length):
    column = jnp.arange(length)[None, :]
    row_index = jnp.arange(length)[:, None]
    offset = column - row_index + fir_taps.shape[0] // 2
    matrix = jnp.zeros((length, length), jnp.float32)
    for tap_index in range(fir_taps.shape[0]):
        matrix = matrix + jnp.where(offset == tap_index, fir_taps[tap_index].astype(jnp.float32), jnp.float32(0.0))
    return matrix.astype(fir_taps.dtype)

def filter_rows(trace_rows, matrix):
    flattened = trace_rows.reshape(-1, trace_rows.shape[-1])
    product = jnp.dot(flattened, matrix, preferred_element_type=jnp.float32)
    return product.astype(jnp.bfloat16).reshape(trace_rows.shape)

def reference(traces, fir_taps, pair_bins, bin_order):
    filtered = filter_rows(traces, fir_matrix(fir_taps, SAMPLES)).astype(jnp.float32)
    padded = jnp.pad(filtered, ((0, 0), (0, 0), (MAXLAG, MAXLAG - 1)))

    def one_block(running, block_index):
        first_row = (block_index * CH_BLOCK).astype(jnp.int32)
        receivers = lax.dynamic_slice_in_dim(padded, first_row, CH_BLOCK, 1)
        labels = lax.dynamic_slice_in_dim(pair_bins, first_row, CH_BLOCK, 1)
        values = lax.conv_general_dilated(receivers, filtered, (1,), 'VALID', dimension_numbers=('CNH', 'IOH', 'CNH'), precision=lax.Precision.HIGHEST, preferred_element_type=jnp.float32)
        running = running + jax.ops.segment_sum(values.reshape(-1, LAGS), labels.reshape(-1), num_segments=NBINS)
        return (running, None)
    start_sums = jnp.zeros((NBINS, LAGS), jnp.float32)
    bin_sums, unused = lax.scan(one_block, start_sums, jnp.arange(CHANNELS // CH_BLOCK, dtype=jnp.int32))
    counts = jax.ops.segment_sum(jnp.ones((CHANNELS * CHANNELS,), jnp.float32), pair_bins.reshape(-1), num_segments=NBINS)
    normalizer = lax.rsqrt(jnp.maximum(counts, 1.0) * (SEGS * SAMPLES))
    stacks = bin_sums * normalizer[:, None]
    return jnp.take(stacks, bin_order, axis=0)
```

```python
import functools

import jax
import jax.numpy as jnp
import ml_dtypes
import numpy as np
from jax import lax
from jax.experimental import pallas as pl
from jax.experimental.pallas import tpu as pltpu
from jax.sharding import PartitionSpec as P

MAXLAG = 64
LAGS = 2 * MAXLAG
BF16, F32 = jnp.bfloat16, jnp.float32
NT = (((1,), (1,)), ((), ()))
NN = (((1,), (0,)), ((), ()))
VMEM_BYTES = 56 * 2**20


def dot(a, b, dims=NN):
    return lax.dot_general(a, b, dims, preferred_element_type=F32)


def exact_dot(a, b):
    return lax.dot_general(a, b, NN, precision=lax.Precision.HIGHEST, preferred_element_type=F32)


def forward_table(length):
    period = length + MAXLAG
    angle = 2 * np.pi / period * (np.arange(period // 2)[:, None] + 0.5) * np.arange(length)[None, :]
    table = np.concatenate([np.cos(angle), -np.sin(angle)], 0)
    high = table.astype(ml_dtypes.bfloat16)
    low = (table - high.astype(np.float64)).astype(ml_dtypes.bfloat16)
    return np.concatenate([high, low], 1)


def inverse_table(length, group, slot, per_tile):
    period = length + MAXLAG
    groups = period // 2 // group
    lag = np.arange(LAGS) - MAXLAG
    table = np.zeros((group, slot, LAGS))
    for g in range(groups):
        angle = 2 * np.pi / period * (g * group + np.arange(group)[:, None] + 0.5) * lag[None, :]
        table[:, 2 * g] = 2 / period * np.cos(angle)
        table[:, 2 * g + 1] = -2 / period * np.sin(angle)
    return table.reshape(group * slot, LAGS).astype(np.float32)


def fir_kernel(half, taps, out):
    length = out.shape[0]
    spread = jnp.broadcast_to(taps[...], (length, length))
    rolled = pltpu.roll(spread, length - half, 1, stride=1, stride_axis=0)
    distance = lax.broadcasted_iota(jnp.int32, (length, length), 1) - lax.broadcasted_iota(
        jnp.int32, (length, length), 0
    )
    out[...] = jnp.where(jnp.abs(distance) <= half, rolled, 0.0).astype(out.dtype)


def fir_matrix(fir_taps, length):
    taps = jnp.pad(fir_taps.astype(F32)[None, :], ((0, 0), (0, length - fir_taps.shape[0])))
    return pl.pallas_call(
        functools.partial(fir_kernel, fir_taps.shape[0] // 2),
        out_shape=jax.ShapeDtypeStruct((length, length), fir_taps.dtype),
        in_specs=[pl.BlockSpec(memory_space=pltpu.VMEM)],
        out_specs=pl.BlockSpec(memory_space=pltpu.VMEM),
        name="fir_matrix",
    )(taps)


def transform(records, matrix, table, width, residues):
    filtered = dot(records, matrix).astype(BF16)
    segs = records.shape[0] // width
    rows = []
    for first in range(0, width, residues):
        rows.append(
            jnp.concatenate(
                [filtered[s * width + first : s * width + first + residues] for s in range(segs)], 0
            )
        )
    lanes = segs * residues
    batch = max(1, 256 // lanes)
    results = []
    for start in range(0, len(rows), batch):
        some = jnp.concatenate(rows[start : start + batch], 0)
        spectra = dot(table, jnp.concatenate([some, some], 1), NT).astype(BF16)
        for index in range(len(rows[start : start + batch])):
            results.append(spectra[:, index * lanes : (index + 1) * lanes])
    return results


def load_block(mine, mate, held, sems):
    rows = mine.shape[0]
    copies = [
        pltpu.make_async_copy(mine, held.at[pl.ds(0, rows)], sems.at[0]),
        pltpu.make_async_copy(mate, held.at[pl.ds(rows, rows)], sems.at[1]),
    ]
    for copy in copies:
        copy.start()
    return copies


def early_kernel(blocks, width, residues, matrix, table, *refs):
    sources, out, held, sems = refs[: 2 * blocks], refs[2 * blocks], refs[2 * blocks + 1], refs[2 * blocks + 2]
    copies = [
        load_block(sources[2 * k], sources[2 * k + 1], held.at[k], sems.at[k]) for k in range(blocks)
    ]
    per_block = width // residues
    for k in range(blocks):
        for copy in copies[k]:
            copy.wait()
        for index, rows in enumerate(transform(held[k], matrix[...], table[...], width, residues)):
            out[k * per_block + index] = rows


def late_kernel(
    width, residues, segs, length, src_count,
    scalars, matrix, table, inverse, ones_zeros, row_bins, early, mine, mate,
    out, held, spectra, edges, shifted, parts, sems, early_sems,
):
    src, shift = scalars[0], scalars[1]
    per_block = width // residues
    rows_q = spectra.shape[0] - 2
    freqs = (length + MAXLAG) // 2
    lanes = segs * residues
    group = 256 // rows_q
    groups = freqs // group
    last = src_count - 1
    loads = load_block(mine, mate, held, sems)
    moves = []
    for k in range(last):
        moves.append(
            pltpu.make_async_copy(
                early.at[pl.ds(k * per_block, per_block)],
                spectra.at[pl.ds(1 + per_block * (src ^ k), per_block), pl.ds(0, 2 * freqs)],
                early_sems.at[k],
            )
        )
        moves[-1].start()
    pad = jnp.zeros((2 * freqs + 16, lanes), BF16)
    spectra[0] = pad
    spectra[rows_q + 1] = pad
    one = jnp.ones((16, lanes), BF16)
    for q in range(rows_q):
        spectra[1 + q, 2 * freqs : 2 * freqs + 16] = one

    jitter = ones_zeros[...]
    blocks, block_lanes = jitter.shape
    edges[...] = jnp.zeros_like(edges)
    per_row = block_lanes // residues
    source_lane = lax.broadcasted_iota(jnp.int32, (block_lanes, lanes), 0)
    target_lane = lax.broadcasted_iota(jnp.int32, (block_lanes, lanes), 1)
    for index in range(per_row):
        pick = (source_lane == target_lane % residues + index * residues).astype(F32)
        spread = exact_dot(jitter, pick)
        for b in range(blocks):
            row = 8 + b * per_row + index
            edges[row : row + 1, :] = spread[b : b + 1, :]
    jitter_rows = edges[8 : 8 + rows_q, :]
    pairs = jnp.concatenate([edges[7:31, :], edges[8:32, :]], 1)
    pairs = jnp.concatenate([pairs, jnp.zeros((104, 2 * lanes), F32)], 0)
    jitter_columns = jnp.concatenate(
        [pairs[:, 128 * i : 128 * (i + 1)].T for i in range(2 * lanes // 128)], 0
    )

    row_lane = lax.broadcasted_iota(jnp.int32, (2 * lanes, lanes), 0)
    col_lane = lax.broadcasted_iota(jnp.int32, (2 * lanes, lanes), 1)
    same_seg = (row_lane % lanes) // residues == col_lane // residues
    place = (row_lane // lanes) * residues + row_lane % residues - col_lane % residues - shift
    here = jnp.where(same_seg & (place == 0), F32(1), F32(0))
    after = jnp.where(same_seg & (place == 1), F32(1), F32(0))
    here_bf = here.astype(BF16)
    difference = here - after

    for copy in loads:
        copy.wait()
    for index, rows in enumerate(transform(held[...], matrix[...], table[...], width, residues)):
        spectra[1 + per_block * (src ^ last) + index, 0 : 2 * freqs] = rows
    for move in moves:
        move.wait()

    for p in range(rows_q + 1):
        mix = after + difference * jitter_columns[:, p : p + 1]
        mapping = jnp.concatenate([here_bf, mix.astype(BF16)], 1)
        both = jnp.concatenate([spectra[p], spectra[p + 1]], 1)
        moved = dot(both, mapping).astype(BF16)
        shifted[p, 0 : 2 * freqs + 16] = moved
        shifted[p, 2 * freqs + 16 : 3 * freqs + 16] = -moved[0:freqs]

    upper = jitter_rows.astype(BF16)
    lower = (1.0 - jitter_rows).astype(BF16)
    freq_row = lax.broadcasted_iota(jnp.int32, (group, 256), 0)
    freq_lane = lax.broadcasted_iota(jnp.int32, (group, 256), 1)
    diagonal = freq_row == freq_lane % group
    slot_lane = lax.broadcasted_iota(jnp.int32, (8, 256), 1) // group

    def gather_bins(block, p, low, high):
        kept = jnp.where(diagonal, block, 0.0)
        total = kept[0:8]
        for i in range(1, group // 8):
            total = total + kept[8 * i : 8 * i + 8]
        amount = (256 - group * p) % 256
        if amount:
            total = pltpu.roll(total, amount, 1)
        if p == 0:
            return low + total, high
        if p == rows_q:
            return low, high + total
        first = slot_lane < rows_q - p
        return low + jnp.where(first, total, 0.0), high + jnp.where(first, 0.0, total)

    zero = jnp.zeros((8, 256), F32)
    parts[...] = jnp.zeros_like(parts)

    def one_group(g, carry):
        first = pl.multiple_of(g * group, group)
        real = pl.ds(first, group)
        imag = pl.ds(first + freqs, group)
        minus = pl.ds(first + 2 * freqs + 16, group)
        left = []
        for q in range(rows_q):
            re, im = spectra[1 + q, real], spectra[1 + q, imag]
            lo, up = lower[q : q + 1], upper[q : q + 1]
            left.append(jnp.concatenate([re * lo, re * up, im * lo, im * up], 1))
        right = []
        for p in range(rows_q + 1):
            re, im, neg = shifted[p, real], shifted[p, imag], shifted[p, minus]
            right.append(jnp.concatenate([re, im], 1))
            right.append(jnp.concatenate([im, neg], 1))
        product = dot(jnp.concatenate(right, 0), jnp.concatenate(left, 0), NT)
        sums = [zero] * 4
        for p in range(rows_q + 1):
            for part in range(2):
                start = (2 * p + part) * group
                sums[2 * part], sums[2 * part + 1] = gather_bins(
                    product[start : start + group], p, sums[2 * part], sums[2 * part + 1]
                )
        for part in range(2):
            for wrap in range(2):
                parts[wrap, pl.ds(2 * g + part, 1), :] = jnp.sum(sums[2 * part + wrap], 0, keepdims=True)
        return carry

    lax.fori_loop(0, groups, one_group, 0)

    count_left = []
    for q in range(rows_q):
        row = jnp.concatenate([lower[q : q + 1], upper[q : q + 1]], 1)
        count_left.append(jnp.broadcast_to(row, (group, 2 * lanes)))
    ones_rows = [shifted[p, 2 * freqs : 2 * freqs + 16] for p in range(rows_q + 1)]
    if group > 16:
        ones_rows = [jnp.concatenate([rows] * (group // 16), 0) for rows in ones_rows]
    counted = dot(jnp.concatenate(ones_rows, 0), jnp.concatenate(count_left, 0), NT)
    count_low, count_high = zero, zero
    for p in range(rows_q + 1):
        count_low, count_high = gather_bins(
            counted[p * group : (p + 1) * group], p, count_low, count_high
        )
    counts = jnp.concatenate(
        [jnp.sum(count_low, 0, keepdims=True), jnp.sum(count_high, 0, keepdims=True)], 1
    )

    used = parts.shape[1]
    per_tile = 128 // used
    freq_of_row = lax.broadcasted_iota(jnp.int32, (256, 128), 0) % group
    tile_slot = lax.broadcasted_iota(jnp.int32, (256, 128), 1) // used
    lagged = []
    for wrap in range(2):
        stacked = jnp.concatenate([parts[wrap]] * per_tile, 0)
        turned = jnp.concatenate([stacked[:, 0:128].T, stacked[:, 128:256].T], 0)
        tiles = [
            jnp.where(freq_of_row == tile_slot + per_tile * i, turned, 0.0)
            for i in range(group // per_tile)
        ]
        lagged.append(exact_dot(jnp.concatenate(tiles, 1), inverse[...]))
    lagged = jnp.concatenate(lagged, 0)

    bins = row_bins[...]
    owned = bins.shape[0]
    lane = lax.broadcasted_iota(jnp.int32, (owned, 512), 1)
    lane_bin = (lane // 256 + 1) * rows_q - 1 - lane % 256 // group
    picked = jnp.concatenate([bins] * 4, 1) == lane_bin
    total = exact_dot(jnp.where(picked, F32(1), F32(0)), lagged)
    count = jnp.sum(jnp.where(picked & (lane % group == 0), counts, 0.0), 1, keepdims=True) / segs
    out[...] = total * lax.rsqrt(jnp.maximum(count, 1.0) * (segs * length))


def partners(axis, step):
    return [(index, index ^ step) for index in range(lax.axis_size(axis))]


def on_device(traces, fir_taps, pair_bins, bin_order):
    seg_local, width, length = traces.shape
    src_count, rcv_count, seg_count = (lax.axis_size(axis) for axis in ("src", "rcv", "seg"))
    segs = seg_local * seg_count
    channels = width * src_count
    owners = src_count * rcv_count * seg_count
    residues = owners
    rows_q = channels // residues
    lanes = segs * residues
    period = length + MAXLAG
    group = 256 // rows_q
    owned = bin_order.shape[0] // owners
    src, rcv = lax.axis_index("src"), lax.axis_index("rcv")

    mine = traces.reshape(seg_local * width, length)
    received = [mine] + [lax.ppermute(mine, "src", partners("src", k)) for k in range(1, src_count)]
    receivers = pair_bins.shape[1]
    jitter = pair_bins[width - 1 : width, :] - (
        rcv * receivers + jnp.arange(receivers, dtype=jnp.int32)[None, :]
    )
    slots = jnp.arange(rcv_count, dtype=jnp.int32)[:, None]
    jitter = jnp.where((slots == rcv) & (src == src_count - 1), jitter, 0).astype(F32)
    for axis, count in (("rcv", rcv_count), ("src", src_count)):
        step = 1
        while step < count:
            jitter = jitter + lax.ppermute(jitter, axis, partners(axis, step))
            step *= 2

    mates = [lax.ppermute(block, "seg", partners("seg", 1)) for block in received]
    matrix = fir_matrix(fir_taps, length)
    table = jnp.asarray(forward_table(length))
    used = 1
    while used < period // group:
        used *= 2
    inverse = jnp.asarray(inverse_table(length, group, used, 128 // used))
    rank = (src * rcv_count + rcv) * seg_count + lax.axis_index("seg")
    own_bins = lax.dynamic_slice_in_dim(bin_order, rank * owned, owned, 0)
    row_bins = jnp.broadcast_to((own_bins // residues)[:, None], (owned, 128))
    scalars = jnp.stack([src, own_bins[0] % residues]).astype(jnp.int32)

    vmem = pl.BlockSpec(memory_space=pltpu.VMEM)
    smem = pl.BlockSpec(memory_space=pltpu.SMEM)
    hbm = pl.BlockSpec(memory_space=pl.ANY)
    last = src_count - 1
    per_block = width // residues
    early = pl.pallas_call(
        functools.partial(early_kernel, last, width, residues),
        out_shape=jax.ShapeDtypeStruct((last * per_block, period, lanes), BF16),
        in_specs=[vmem, vmem] + [hbm] * (2 * last),
        out_specs=vmem,
        scratch_shapes=[
            pltpu.VMEM((last, segs * width, length), BF16),
            pltpu.SemaphoreType.DMA((last, 2)),
        ],
        compiler_params=pltpu.CompilerParams(vmem_limit_bytes=VMEM_BYTES),
        name="early_spectra",
    )(matrix, table, *[a for k in range(last) for a in (received[k], mates[k])])
    return pl.pallas_call(
        functools.partial(late_kernel, width, residues, segs, length, src_count),
        out_shape=jax.ShapeDtypeStruct((owned, LAGS), F32),
        in_specs=[smem] + [vmem] * 5 + [hbm] * 3,
        out_specs=vmem,
        scratch_shapes=[
            pltpu.VMEM((segs * width, length), BF16),
            pltpu.VMEM((rows_q + 2, period + 16, lanes), BF16),
            pltpu.VMEM((32, lanes), F32),
            pltpu.VMEM((rows_q + 1, period + 16 + period // 2, 2 * lanes), BF16),
            pltpu.VMEM((2, used, 256), F32),
            pltpu.SemaphoreType.DMA((2,)),
            pltpu.SemaphoreType.DMA((last,)),
        ],
        compiler_params=pltpu.CompilerParams(vmem_limit_bytes=VMEM_BYTES),
        name="bin_stacks",
    )(scalars, matrix, table, inverse, jitter, row_bins, early, received[last], mates[last])


def solution(mesh):
    return jax.shard_map(
        on_device,
        mesh=mesh,
        in_specs=(P("seg", "src", None), P(), P("src", "rcv"), P()),
        out_specs=P(("src", "rcv", "seg"), None),
        check_vma=False,
    )
```

```python
import functools

import jax
import jax.numpy as jnp
import ml_dtypes
import numpy as np
from jax import lax
from jax.experimental import pallas as pl
from jax.experimental.pallas import tpu as pltpu
from jax.sharding import PartitionSpec as P

MAXLAG = 64
LAGS = 2 * MAXLAG
BF16, F32 = jnp.bfloat16, jnp.float32
NT = (((1,), (1,)), ((), ()))
NN = (((1,), (0,)), ((), ()))
UNROLL = 36


def dot(a, b, dims=NN):
    return lax.dot_general(a, b, dims, preferred_element_type=F32)


def exact_dot(a, b):
    return lax.dot_general(a, b, NN, precision=lax.Precision.HIGHEST, preferred_element_type=F32)


def frequencies(length):
    period = length + MAXLAG
    return 2 * np.pi / period * (np.arange(period // 2) + 0.5)


def angle_parts(length, group):
    width = length + MAXLAG
    first, time = frequencies(length)[:group], np.arange(length)
    stride = frequencies(length)[::group] - first[0]
    column = np.repeat(frequencies(length).reshape(-1, 1, group), 2, 1).reshape(-1)
    parts = []
    for angle in (stride[:, None] * time, first[:, None] * time):
        parts += [np.pad(table, ((0, 0), (0, MAXLAG))) for table in (np.cos(angle), np.sin(angle))]
    for lag in (np.arange(-MAXLAG, MAXLAG, 8), np.arange(8)):
        angle = lag[:, None] * column
        parts += [np.cos(angle), np.sin(angle)]
    assert all(part.shape[1] == width for part in parts)
    return np.concatenate([np.pad(p, ((0, -p.shape[0] % 8), (0, 0))) for p in parts]).astype(np.float32)


def store_halves(ref, rows, value, times):
    width = value.shape[1]
    high = value.astype(BF16)
    low = (value - high.astype(F32)).astype(BF16)
    order = (high, low) if times == 2 else (high, high, low)
    ref[rows] = jnp.concatenate(order, 1)


def prepare_kernel(half, group, taps, parts, matrix_t, table, inverse):
    length = matrix_t.shape[0]
    row = jnp.concatenate([taps[...].astype(F32), jnp.zeros((1, length - taps.shape[1]), F32)], 1)
    spread = jnp.broadcast_to(row, (length, length))
    rolled = pltpu.roll(spread, length - half, 1, stride=1, stride_axis=0).T
    distance = lax.broadcasted_iota(jnp.int32, (length, length), 1) - lax.broadcasted_iota(
        jnp.int32, (length, length), 0
    )
    matrix_t[...] = jnp.where(jnp.abs(distance) <= half, rolled, 0.0).astype(matrix_t.dtype)

    groups = (length + MAXLAG) // 2 // group
    padded = groups + -groups % 8
    cos_first, sin_first = (parts[2 * padded + i * group : 2 * padded + (i + 1) * group, 0:length] for i in range(2))
    for g in range(groups):
        cos_step, sin_step = parts[g : g + 1, 0:length], parts[padded + g : padded + g + 1, 0:length]
        real = cos_first * cos_step - sin_first * sin_step
        imag = -(sin_first * cos_step + cos_first * sin_step)
        store_halves(table, pl.ds(2 * g * group, 2 * group), jnp.concatenate([real, imag], 0), 2)

    base = 2 * padded + 2 * group
    steps = LAGS // 8
    cos_first, sin_first = (parts[base + 2 * steps + 8 * i : base + 2 * steps + 8 * (i + 1), :] for i in range(2))
    lane = lax.broadcasted_iota(jnp.int32, (8, length + MAXLAG), 1)
    is_real = (lane & group) == 0
    scale = F32(2.0 / (length + MAXLAG))
    for step in range(steps):
        cos_step = parts[base + step : base + step + 1, :] * scale
        sin_step = parts[base + steps + step : base + steps + step + 1, :] * scale
        cosine = cos_first * cos_step - sin_first * sin_step
        sine = sin_first * cos_step + cos_first * sin_step
        store_halves(inverse, pl.ds(8 * step, 8), jnp.where(is_real, cosine, -sine), 3)
        store_halves(inverse, pl.ds(LAGS + 8 * step, 8), jnp.where(is_real, sine, cosine), 3)


def transform(records, matrix_t, table, width, residues):
    segs = records.shape[0] // width
    rows = [
        records[s * width + first : s * width + first + residues]
        for first in range(0, width, residues)
        for s in range(segs)
    ]
    filtered = dot(matrix_t, jnp.concatenate(rows, 0), NT).astype(BF16)
    return dot(table, jnp.concatenate([filtered, filtered], 0)).astype(BF16)


def block_kernel(width, residues, matrix_t, table, mine, mate, out):
    records = jnp.concatenate([mine[...], mate[...]], 0)
    spectra = transform(records, matrix_t[...], table[...], width, residues)
    lanes = out.shape[2]
    for index in range(out.shape[0]):
        out[index] = spectra[:, index * lanes : (index + 1) * lanes]


def bin_lanes(product, first_row, rows_per, group, rows_q):
    width = 256 // rows_q
    per = 128 // width
    lane = lax.broadcasted_iota(jnp.int32, (group, 128), 1)

    def tile(p, half):
        start = p * rows_per + first_row
        return product[start : start + group, 128 * half : 128 * half + 128]

    total = [tile(2 * per, 0), tile(per, 0) + tile(2 * per, 1), tile(0, 0) + tile(per, 1), tile(0, 1)]
    for p in range(1, per):
        kept = width * (per - p)
        moved = [
            pltpu.roll(part, kept, 1)
            for part in (tile(per + p, 0), tile(p, 0) + tile(per + p, 1), tile(p, 1))
        ]
        inside = lane < kept
        total[0] = total[0] + jnp.where(inside, 0.0, moved[0])
        total[1] = total[1] + jnp.where(inside, moved[0], moved[1])
        total[2] = total[2] + jnp.where(inside, moved[1], moved[2])
        total[3] = total[3] + jnp.where(inside, moved[2], 0.0)
    place = lax.broadcasted_iota(jnp.int32, (group, 128), 0)
    diagonal = place == (lane & (group - 1))
    return jnp.concatenate([jnp.where(diagonal, part, 0.0) for part in total], 1)


def late_kernel(
    width, residues, segs, length, src_count,
    jitter_ref, arrived, bin_order, matrix_t, table, inverse, *refs,
):
    early, refs = refs[: src_count - 1], refs[src_count - 1 :]
    mine, mate, out, spectra, edges, shifted, binned = refs
    src = lax.axis_index("src")
    owned = out.shape[0]
    rank = lax.axis_index(("src", "rcv", "seg"))
    per_line = 128 // owned
    order = pltpu.roll(bin_order[pl.ds(rank // per_line, 1), :], 128 - owned * (rank % per_line), 1)
    square = (owned, 128)
    same = lax.broadcasted_iota(jnp.int32, square, 0) == lax.broadcasted_iota(jnp.int32, square, 1)
    bins = jnp.sum(jnp.where(same, jnp.broadcast_to(order, square), 0), 1, keepdims=True)
    shift = bins[0:1, 0:1] & (residues - 1)
    per_block = width // residues
    rows_q = spectra.shape[0] - 2
    height = length + MAXLAG
    lanes = segs * residues
    step = 256 // rows_q
    group = step // 2
    last = src_count - 1
    pad = jnp.zeros((height + 16, lanes), BF16)
    spectra[0] = pad
    spectra[rows_q + 1] = pad
    one = jnp.ones((16, lanes), BF16)
    for q in range(rows_q):
        spectra[1 + q, height : height + 16] = one

    jitter = jitter_ref[...] + arrived[...]
    blocks, block_lanes = jitter.shape
    edges[...] = jnp.zeros_like(edges)
    source_lane = lax.broadcasted_iota(jnp.int32, (block_lanes, lanes), 0)
    target_lane = lax.broadcasted_iota(jnp.int32, (block_lanes, lanes), 1) & (residues - 1)
    per_row = block_lanes // residues
    for index in range(per_row):
        pick = jnp.where(source_lane == target_lane + index * residues, F32(1), F32(0))
        spread = dot(jitter.astype(BF16), pick.astype(BF16))
        for b in range(blocks):
            row = 8 + b * per_row + index
            edges[row : row + 1, :] = spread[b : b + 1, :]
    jitter_rows = edges[8 : 8 + rows_q, :]
    pairs = jnp.concatenate([edges[7:31, :], edges[8:32, :]], 1)
    pairs = jnp.concatenate([pairs, jnp.zeros((104, 2 * lanes), F32)], 0)
    jitter_columns = jnp.concatenate(
        [pairs[:, 128 * i : 128 * (i + 1)].T for i in range(2 * lanes // 128)], 0
    )

    row_lane = lax.broadcasted_iota(jnp.int32, (2 * lanes, lanes), 0)
    col_lane = lax.broadcasted_iota(jnp.int32, (2 * lanes, lanes), 1)
    bits = residues.bit_length() - 1
    same_seg = ((row_lane & (lanes - 1)) >> bits) == (col_lane >> bits)
    inside = (row_lane & (residues - 1)) - (col_lane & (residues - 1)) - shift
    place = inside + jnp.where(row_lane >= lanes, residues, 0)
    here = jnp.where(same_seg & (place == 0), F32(1), F32(0))
    after = jnp.where(same_seg & (place == 1), F32(1), F32(0))
    here_bf = here.astype(BF16)
    difference = here - after

    records = jnp.concatenate([mine[...], mate[...]], 0)
    fresh = transform(records, matrix_t[...], table[...], width, residues)
    for index in range(per_block):
        spectra[1 + per_block * (src ^ last) + index, 0:height] = fresh[:, index * lanes : (index + 1) * lanes]
    for k in range(last):
        for index in range(per_block):
            spectra[1 + per_block * (src ^ k) + index, 0:height] = early[k][index]

    for p in range(rows_q + 1):
        mix = after + difference * jitter_columns[:, p : p + 1]
        mapping = jnp.concatenate([here_bf, mix.astype(BF16)], 1)
        both = jnp.concatenate([spectra[p], spectra[p + 1]], 1)
        shifted[p] = dot(both, mapping).astype(BF16)

    upper = jitter_rows.astype(BF16)
    lower = (1.0 - jitter_rows).astype(BF16)

    def one_group(g, carry):
        rows = pl.ds(pl.multiple_of(g * step, step), step)
        left = []
        for q in range(rows_q):
            values = spectra[1 + q, rows]
            left.append(jnp.concatenate([values * lower[q : q + 1], values * upper[q : q + 1]], 1))
        right = [shifted[p, rows] for p in range(rows_q + 1)]
        product = dot(jnp.concatenate(right, 0), jnp.concatenate(left, 0), NT)
        binned[rows] = jnp.concatenate(
            [bin_lanes(product, part * group, step, group, rows_q) for part in range(2)], 0
        )
        return carry

    lax.fori_loop(0, height // step, one_group, 0, unroll=UNROLL)

    count_left = []
    for q in range(rows_q):
        row = jnp.concatenate([lower[q : q + 1], upper[q : q + 1]], 1)
        count_left.append(jnp.broadcast_to(row, (step, 2 * lanes)))
    ones_rows = [shifted[p, height : height + 16] for p in range(rows_q + 1)]
    counted = dot(jnp.concatenate(ones_rows, 0), jnp.concatenate(count_left, 0), NT)
    if group > 8:
        counted = jnp.concatenate([counted[16 * p : 16 * p + 16] for p in range(rows_q + 1)], 0)
    counts = jnp.sum(bin_lanes(counted, 0, 16, group, rows_q), 0, keepdims=True)

    values = binned[...]
    high = values.astype(BF16)
    low = (values - high.astype(F32)).astype(BF16)
    lagged = dot(inverse[...], jnp.concatenate([high, low, high], 0))
    lane = lax.broadcasted_iota(jnp.int32, (LAGS, 512), 1)
    lagged = jnp.where((lane & group) == 0, lagged[0:LAGS], lagged[LAGS:])
    high = lagged.astype(BF16)
    low = (lagged - high.astype(F32)).astype(BF16)

    lane = lax.broadcasted_iota(jnp.int32, (owned, 512), 1)
    lane_bin = 2 * rows_q - 1 - (lane >> (step.bit_length() - 1))
    picked = (bins >> (residues.bit_length() - 1)) == lane_bin
    weights = jnp.where(picked, F32(1), F32(0))
    total = dot(
        jnp.concatenate([weights, weights], 1).astype(BF16), jnp.concatenate([high, low], 1), NT
    )
    count = jnp.sum(jnp.where((lane & (step - 1)) == 0, weights * counts, 0.0), 1, keepdims=True) / segs
    out[...] = total * lax.rsqrt(jnp.maximum(count, 1.0) * (segs * length))


def cost(microseconds):
    return pl.CostEstimate(
        flops=int(microseconds * 1e9), bytes_accessed=int(microseconds * 3e6), transcendentals=0
    )


def partners(axis, step):
    return [(index, index ^ step) for index in range(lax.axis_size(axis))]


def on_device(traces, fir_taps, pair_bins, bin_order):
    seg_local, width, length = traces.shape
    src_count, rcv_count, seg_count = (lax.axis_size(axis) for axis in ("src", "rcv", "seg"))
    segs = seg_local * seg_count
    channels = width * src_count
    owners = src_count * rcv_count * seg_count
    residues = owners
    rows_q = channels // residues
    lanes = segs * residues
    period = length + MAXLAG
    owned = bin_order.shape[0] // owners

    mine = traces.reshape(seg_local * width, length)
    received = [mine] + [lax.ppermute(mine, "src", partners("src", k)) for k in range(1, src_count)]
    mates = [lax.ppermute(mine, "seg", partners("seg", 1))]

    src, rcv = lax.axis_index("src"), lax.axis_index("rcv")
    receivers = pair_bins.shape[1]
    jitter = pair_bins[width - 1 : width, :] - (
        rcv * receivers + jnp.arange(receivers, dtype=jnp.int32)[None, :]
    )
    slots = jnp.arange(rcv_count, dtype=jnp.int32)[:, None]
    jitter = jnp.where((slots == rcv) & (src == src_count - 1), jitter, 0).astype(F32)

    vmem = pl.BlockSpec(memory_space=pltpu.VMEM)
    last = src_count - 1
    per_block = width // residues
    params = pltpu.CompilerParams(vmem_limit_bytes=(20 if lanes <= 128 else 40) * 2**20)
    group = 128 // rows_q
    matrix_t, table, inverse = pl.pallas_call(
        functools.partial(prepare_kernel, fir_taps.shape[0] // 2, group),
        out_shape=[
            jax.ShapeDtypeStruct((length, length), BF16),
            jax.ShapeDtypeStruct((period, 2 * length), BF16),
            jax.ShapeDtypeStruct((2 * LAGS, 3 * period), BF16),
        ],
        in_specs=[vmem] * 2,
        out_specs=[vmem] * 3,
        compiler_params=params,
        cost_estimate=cost(0.01),
        name="prepare",
    )(fir_taps[None, :], jnp.asarray(angle_parts(length, group)))

    def block_spectra(k):
        return pl.pallas_call(
            functools.partial(block_kernel, width, residues),
            out_shape=jax.ShapeDtypeStruct((per_block, period, lanes), BF16),
            in_specs=[vmem] * 4,
            out_specs=vmem,
            compiler_params=params,
            cost_estimate=cost(0.01),
            name="block_spectra",
        )(matrix_t, table, received[k], mates[k])

    hops = [("rcv", 1 << bit) for bit in range((rcv_count - 1).bit_length())]
    hops += [("src", 1 << bit) for bit in range((src_count - 1).bit_length())]
    arrived = jnp.zeros_like(jitter)
    early = [block_spectra(0)]
    for turn, (axis, step) in enumerate(hops):
        if turn == len(hops) - 1:
            *received[1:], early[0], arrived = lax.optimization_barrier((*received[1:], early[0], arrived))
            mates += [lax.ppermute(block, "seg", partners("seg", 1)) for block in received[1:]]
        jitter = jitter + arrived
        arrived = lax.ppermute(jitter, axis, partners(axis, step))
    early += [block_spectra(k) for k in range(1, last)]
    return pl.pallas_call(
        functools.partial(late_kernel, width, residues, segs, length, src_count),
        out_shape=jax.ShapeDtypeStruct((owned, LAGS), F32),
        in_specs=[vmem] * (last + 8),
        out_specs=vmem,
        scratch_shapes=[
            pltpu.VMEM((rows_q + 2, period + 16, lanes), BF16),
            pltpu.VMEM((32, lanes), F32),
            pltpu.VMEM((rows_q + 1, period + 16, 2 * lanes), BF16),
            pltpu.VMEM((period, 512), F32),
        ],
        compiler_params=params,
        cost_estimate=cost(0.01),
        name="bin_stacks",
    )(jitter, arrived, bin_order.reshape(-1, 128), matrix_t, table, inverse, *early, received[last], mates[last])


def solution(mesh):
    return jax.shard_map(
        on_device,
        mesh=mesh,
        in_specs=(P("seg", "src", None), P(), P("src", "rcv"), P()),
        out_specs=P(("src", "rcv", "seg"), None),
        check_vma=False,
    )
```

```python
import functools

import jax
import jax.numpy as jnp
import numpy as np
from jax import lax
from jax.experimental import pallas as pl
from jax.experimental.pallas import tpu as pltpu
from jax.sharding import PartitionSpec as P

MAXLAG = 64
LAGS = 2 * MAXLAG
BF16, F32 = jnp.bfloat16, jnp.float32
NT = (((1,), (1,)), ((), ()))
NN = (((1,), (0,)), ((), ()))
UNROLL = 36


def dot(a, b, dims=NN):
    return lax.dot_general(a, b, dims, preferred_element_type=F32)


def exact_dot(a, b):
    return lax.dot_general(a, b, NN, precision=lax.Precision.HIGHEST, preferred_element_type=F32)


def turns(first, second, period):
    product = (first * second).astype(F32)
    whole = jnp.floor((product + 0.5) * F32(0.5 / period))
    angle = (product - whole * F32(2 * period) - F32(period)) * F32(np.pi / period)
    return -jnp.cos(angle), -jnp.sin(angle)


def store_halves(ref, rows, value, times):
    width = value.shape[1]
    high = value.astype(BF16)
    low = (value - high.astype(F32)).astype(BF16)
    order = (high, low) if times == 2 else (high, high, low)
    ref[rows] = jnp.concatenate(order, 1)


def fill_tables(taps, matrix_t, table, inverse, half, group):
    length = matrix_t.shape[0]
    period = length + MAXLAG
    row = jnp.concatenate([taps[...].astype(F32), jnp.zeros((1, length - taps.shape[1]), F32)], 1)
    spread = jnp.broadcast_to(row, (length, length))
    rolled = pltpu.roll(spread, length - half, 1, stride=1, stride_axis=0).T
    distance = lax.broadcasted_iota(jnp.int32, (length, length), 1) - lax.broadcasted_iota(
        jnp.int32, (length, length), 0
    )
    matrix_t[...] = jnp.where(jnp.abs(distance) <= half, rolled, 0.0).astype(matrix_t.dtype)

    def iota(shape, dim):
        return lax.broadcasted_iota(jnp.int32, shape, dim)

    groups = period // 2 // group
    padded = groups + -groups % 8
    cos_first, sin_first = turns(2 * iota((group, length), 0) + 1, iota((group, length), 1), period)
    cos_steps, sin_steps = turns(2 * group * iota((padded, length), 0), iota((padded, length), 1), period)
    for g in range(groups):
        cos_step, sin_step = cos_steps[g : g + 1], sin_steps[g : g + 1]
        real = cos_first * cos_step - sin_first * sin_step
        imag = -(sin_first * cos_step + cos_first * sin_step)
        store_halves(table, pl.ds(2 * g * group, 2 * group), jnp.concatenate([real, imag], 0), 2)

    steps = LAGS // 8
    half_period = period // 2

    def odd(rows):
        return 2 * iota((rows, half_period), 1) + 1

    cos_first, sin_first = turns(odd(8), iota((8, half_period), 0), period)
    cos_steps, sin_steps = turns(odd(steps), 8 * iota((steps, half_period), 0) + 2 * period - MAXLAG, period)
    scale = F32(2.0 / period)
    cos_steps, sin_steps = cos_steps * scale, sin_steps * scale
    for step in range(steps):
        cos_step, sin_step = cos_steps[step : step + 1], sin_steps[step : step + 1]
        cosine = cos_first * cos_step - sin_first * sin_step
        sine = sin_first * cos_step + cos_first * sin_step
        store_halves(inverse, pl.ds(8 * step, 8), cosine, 3)
        store_halves(inverse, pl.ds(LAGS + 8 * step, 8), sine, 3)


def first_kernel(half, group, width, residues, taps, mine, mate, matrix_t, table, inverse, out):
    fill_tables(taps, matrix_t, table, inverse, half, group)
    block_kernel(width, residues, matrix_t, table, mine, mate, out)


def transform(records, matrix_t, table, width, residues):
    segs = records.shape[0] // width
    rows = [
        records[s * width + first : s * width + first + residues]
        for first in range(0, width, residues)
        for s in range(segs)
    ]
    filtered = dot(matrix_t, jnp.concatenate(rows, 0), NT).astype(BF16)
    return dot(table, jnp.concatenate([filtered, filtered], 0)).astype(BF16)


def block_kernel(width, residues, matrix_t, table, *refs):
    count = len(refs) // 3
    for mine, mate, out in zip(refs[:count], refs[count : 2 * count], refs[2 * count :]):
        records = jnp.concatenate([mine[...], mate[...]], 0)
        spectra = transform(records, matrix_t[...], table[...], width, residues)
        lanes = out.shape[2]
        for index in range(out.shape[0]):
            out[index] = spectra[:, index * lanes : (index + 1) * lanes]


def bin_lanes(product, first_row, rows_per, group, rows_q):
    width = 256 // rows_q
    per = 128 // width
    lane = lax.broadcasted_iota(jnp.int32, (group, 128), 1)

    def tile(p, half):
        start = p * rows_per + first_row
        return product[start : start + group, 128 * half : 128 * half + 128]

    total = [tile(2 * per, 0), tile(per, 0) + tile(2 * per, 1), tile(0, 0) + tile(per, 1), tile(0, 1)]
    for p in range(1, per):
        kept = width * (per - p)
        moved = [
            pltpu.roll(part, kept, 1)
            for part in (tile(per + p, 0), tile(p, 0) + tile(per + p, 1), tile(p, 1))
        ]
        inside = lane < kept
        total[0] = total[0] + jnp.where(inside, 0.0, moved[0])
        total[1] = total[1] + jnp.where(inside, moved[0], moved[1])
        total[2] = total[2] + jnp.where(inside, moved[1], moved[2])
        total[3] = total[3] + jnp.where(inside, moved[2], 0.0)
    place = lax.broadcasted_iota(jnp.int32, (group, 128), 0)
    diagonal = place == (lane & (group - 1))
    return jnp.concatenate([jnp.where(diagonal, part, 0.0) for part in total], 1)


def late_kernel(
    width, residues, segs, length, src_count,
    bin_order, matrix_t, table, inverse, *refs,
):
    jitters, early, refs = refs[:2], refs[2 : src_count + 1], refs[src_count + 1 :]
    *pieces, out, spectra, edges, shifted, binned = refs
    src = lax.axis_index("src")
    owned = out.shape[0]
    rank = lax.axis_index(("src", "rcv", "seg"))
    per_line = 128 // owned
    order = pltpu.roll(bin_order[pl.ds(rank // per_line, 1), :], 128 - owned * (rank % per_line), 1)
    square = (owned, 128)
    same = lax.broadcasted_iota(jnp.int32, square, 0) == lax.broadcasted_iota(jnp.int32, square, 1)
    bins = jnp.sum(jnp.where(same, jnp.broadcast_to(order, square), 0), 1, keepdims=True)
    shift = bins[0:1, 0:1] & (residues - 1)
    per_block = width // residues
    rows_q = spectra.shape[0] - 2
    height = length + MAXLAG
    lanes = segs * residues
    step = 256 // rows_q
    group = step // 2
    last = src_count - 1
    pad = jnp.zeros((height + 16, lanes), BF16)
    spectra[0] = pad
    spectra[rows_q + 1] = pad
    one = jnp.ones((16, lanes), BF16)
    for q in range(rows_q):
        spectra[1 + q, height : height + 16] = one

    jitter = sum(ref[...] for ref in jitters)
    blocks, block_lanes = jitter.shape
    edges[...] = jnp.zeros_like(edges)
    source_lane = lax.broadcasted_iota(jnp.int32, (block_lanes, lanes), 0)
    target_lane = lax.broadcasted_iota(jnp.int32, (block_lanes, lanes), 1) & (residues - 1)
    per_row = block_lanes // residues
    for index in range(per_row):
        pick = jnp.where(source_lane == target_lane + index * residues, F32(1), F32(0))
        spread = dot(jitter.astype(BF16), pick.astype(BF16))
        for b in range(blocks):
            row = 8 + b * per_row + index
            edges[row : row + 1, :] = spread[b : b + 1, :]
    jitter_rows = edges[8 : 8 + rows_q, :]
    pairs = jnp.concatenate([edges[7:31, :], edges[8:32, :]], 1)
    pairs = jnp.concatenate([pairs, jnp.zeros((104, 2 * lanes), F32)], 0)
    jitter_columns = jnp.concatenate(
        [pairs[:, 128 * i : 128 * (i + 1)].T for i in range(2 * lanes // 128)], 0
    )

    row_lane = lax.broadcasted_iota(jnp.int32, (2 * lanes, lanes), 0)
    col_lane = lax.broadcasted_iota(jnp.int32, (2 * lanes, lanes), 1)
    bits = residues.bit_length() - 1
    same_seg = ((row_lane & (lanes - 1)) >> bits) == (col_lane >> bits)
    inside = (row_lane & (residues - 1)) - (col_lane & (residues - 1)) - shift
    place = inside + jnp.where(row_lane >= lanes, residues, 0)
    here = jnp.where(same_seg & (place == 0), F32(1), F32(0))
    after = jnp.where(same_seg & (place == 1), F32(1), F32(0))
    here_bf = here.astype(BF16)
    difference = here - after

    records = jnp.concatenate([piece[...] for piece in pieces], 0)
    fresh = transform(records, matrix_t[...], table[...], width, residues)
    for index in range(per_block):
        spectra[1 + per_block * (src ^ last) + index, 0:height] = fresh[:, index * lanes : (index + 1) * lanes]
    for k in range(last):
        for index in range(per_block):
            spectra[1 + per_block * (src ^ k) + index, 0:height] = early[k][index]

    for p in range(rows_q + 1):
        mix = after + difference * jitter_columns[:, p : p + 1]
        mapping = jnp.concatenate([here_bf, mix.astype(BF16)], 1)
        both = jnp.concatenate([spectra[p], spectra[p + 1]], 1)
        shifted[p] = dot(both, mapping).astype(BF16)

    upper = jitter_rows.astype(BF16)
    lower = (1.0 - jitter_rows).astype(BF16)

    swap = (lax.broadcasted_iota(jnp.int32, (height // 2, 128), 1) & group) == 0

    def cross(imag):
        tiles = [imag[:, 128 * i : 128 * (i + 1)] for i in range(4)]
        return jnp.concatenate(
            [jnp.where(swap, pltpu.roll(tile, 128 - group, 1), -pltpu.roll(tile, group, 1)) for tile in tiles], 1
        )

    def one_group(g, carry):
        rows = pl.ds(pl.multiple_of(g * step, step), step)
        left = []
        for q in range(rows_q):
            values = spectra[1 + q, rows]
            left.append(jnp.concatenate([values * lower[q : q + 1], values * upper[q : q + 1]], 1))
        right = [shifted[p, rows] for p in range(rows_q + 1)]
        product = dot(jnp.concatenate(right, 0), jnp.concatenate(left, 0), NT)
        for part in range(2):
            place = pl.ds(pl.multiple_of(g * group, group), group)
            binned[part, place] = bin_lanes(product, part * group, step, group, rows_q)
        return carry

    lax.fori_loop(0, height // step, one_group, 0, unroll=UNROLL)

    count_left = []
    for q in range(rows_q):
        row = jnp.concatenate([lower[q : q + 1], upper[q : q + 1]], 1)
        count_left.append(jnp.broadcast_to(row, (step, 2 * lanes)))
    ones_rows = [shifted[p, height : height + 16] for p in range(rows_q + 1)]
    counted = dot(jnp.concatenate(ones_rows, 0), jnp.concatenate(count_left, 0), NT)
    if group > 8:
        counted = jnp.concatenate([counted[16 * p : 16 * p + 16] for p in range(rows_q + 1)], 0)
    counts = jnp.sum(bin_lanes(counted, 0, 16, group, rows_q), 0, keepdims=True)

    values = binned[0] + cross(binned[1])
    high = values.astype(BF16)
    low = (values - high.astype(F32)).astype(BF16)
    lagged = dot(inverse[...], jnp.concatenate([high, low, high], 0))
    lane = lax.broadcasted_iota(jnp.int32, (LAGS, 512), 1)
    lagged = jnp.where((lane & group) == 0, lagged[0:LAGS], lagged[LAGS:])
    high = lagged.astype(BF16)
    low = (lagged - high.astype(F32)).astype(BF16)

    lane = lax.broadcasted_iota(jnp.int32, (owned, 512), 1)
    lane_bin = 2 * rows_q - 1 - (lane >> (step.bit_length() - 1))
    picked = (bins >> (residues.bit_length() - 1)) == lane_bin
    weights = jnp.where(picked, F32(1), F32(0))
    total = dot(
        jnp.concatenate([weights, weights], 1).astype(BF16), jnp.concatenate([high, low], 1), NT
    )
    count = jnp.sum(jnp.where((lane & (step - 1)) == 0, weights * counts, 0.0), 1, keepdims=True) / segs
    out[...] = total * lax.rsqrt(jnp.maximum(count, 1.0) * (segs * length))


def cost(microseconds):
    return pl.CostEstimate(
        flops=int(microseconds * 1e9), bytes_accessed=int(microseconds * 3e6), transcendentals=0
    )


def partners(axis, step):
    return [(index, index ^ step) for index in range(lax.axis_size(axis))]


def on_device(traces, fir_taps, pair_bins, bin_order):
    seg_local, width, length = traces.shape
    src_count, rcv_count, seg_count = (lax.axis_size(axis) for axis in ("src", "rcv", "seg"))
    segs = seg_local * seg_count
    channels = width * src_count
    owners = src_count * rcv_count * seg_count
    residues = owners
    rows_q = channels // residues
    lanes = segs * residues
    period = length + MAXLAG
    owned = bin_order.shape[0] // owners

    mine = traces.reshape(seg_local * width, length)
    def to_mate(piece):
        return lax.ppermute(piece, "seg", partners("seg", 1))

    received = [mine] + [lax.ppermute(mine, "src", partners("src", k)) for k in range(1, src_count)]
    mates = [to_mate(mine)]

    src, rcv = lax.axis_index("src"), lax.axis_index("rcv")
    assert src_count == rcv_count
    channel = jnp.arange(width, dtype=jnp.int32)[None, :]
    of_receivers = pair_bins[width - 1 : width, :] - (rcv * width + channel)
    of_sources = channels - (src * width + channel) - pair_bins[:, 0:1].reshape(1, width)
    slots = jnp.arange(rcv_count, dtype=jnp.int32)[:, None]
    jitter = jnp.where((slots == rcv) & (src == src_count - 1), of_receivers, 0)
    jitter = (jitter + jnp.where((slots == src) & (rcv == 0), of_sources, 0)).astype(F32)

    vmem = pl.BlockSpec(memory_space=pltpu.VMEM)
    last = src_count - 1
    per_block = width // residues
    params = pltpu.CompilerParams(vmem_limit_bytes=(20 if lanes <= 128 else 40) * 2**20)
    group = 128 // rows_q
    matrix_t, table, inverse, first = pl.pallas_call(
        functools.partial(first_kernel, fir_taps.shape[0] // 2, group, width, residues),
        out_shape=[
            jax.ShapeDtypeStruct((length, length), BF16),
            jax.ShapeDtypeStruct((period, 2 * length), BF16),
            jax.ShapeDtypeStruct((2 * LAGS, 3 * period // 2), BF16),
            jax.ShapeDtypeStruct((per_block, period, lanes), BF16),
        ],
        in_specs=[vmem] * 3,
        out_specs=[vmem] * 4,
        compiler_params=params,
        cost_estimate=cost(0.01),
        name="tables_and_own_spectra",
    )(fir_taps[None, :], mine, mates[0])

    def block_spectra(blocks):
        return pl.pallas_call(
            functools.partial(block_kernel, width, residues),
            out_shape=[jax.ShapeDtypeStruct((per_block, period, lanes), BF16) for _ in blocks],
            in_specs=[vmem] * (2 + 2 * len(blocks)),
            out_specs=[vmem] * len(blocks),
            compiler_params=params,
            cost_estimate=cost(0.01),
            name="block_spectra",
        )(matrix_t, table, *[received[k] for k in blocks], *[mates[k] for k in blocks])

    bits = [1 << bit for bit in range(1, (src_count - 1).bit_length())]
    hops = [(0, bit) for bit in bits] + [(1, 1)] + [(bit, 0) for bit in bits]
    arrived = jnp.zeros_like(jitter)
    for turn, (over_src, over_rcv) in enumerate(hops):
        if turn == len(hops) - 2:
            arrived, first = lax.optimization_barrier((arrived, first))
        if turn == len(hops) - 1:
            *received[1:], first, arrived = lax.optimization_barrier((*received[1:], first, arrived))
        jitter = jitter + arrived
        pairs = [
            (i * rcv_count + z, (i ^ over_src) * rcv_count + (z ^ over_rcv))
            for i in range(src_count)
            for z in range(rcv_count)
        ]
        arrived = lax.ppermute(jitter, ("src", "rcv"), pairs)
    jitters = [jitter, arrived]
    mates += [to_mate(block) for block in received[1:]]
    early = [first, *block_spectra(range(1, last))]
    return pl.pallas_call(
        functools.partial(late_kernel, width, residues, segs, length, src_count),
        out_shape=jax.ShapeDtypeStruct((owned, LAGS), F32),
        in_specs=[vmem] * (last + 8),
        out_specs=vmem,
        scratch_shapes=[
            pltpu.VMEM((rows_q + 2, period + 16, lanes), BF16),
            pltpu.VMEM((32, lanes), F32),
            pltpu.VMEM((rows_q + 1, period + 16, 2 * lanes), BF16),
            pltpu.VMEM((2, period // 2, 512), F32),
        ],
        compiler_params=params,
        cost_estimate=cost(0.01),
        name="bin_stacks",
    )(bin_order.reshape(-1, 128), matrix_t, table, inverse, *jitters, *early, received[last], mates[last])


def solution(mesh):
    return jax.shard_map(
        on_device,
        mesh=mesh,
        in_specs=(P("seg", "src", None), P(), P("src", "rcv"), P()),
        out_specs=P(("src", "rcv", "seg"), None),
        check_vma=False,
    )
```

```python
import functools

import jax
import jax.numpy as jnp
import numpy as np
from jax import lax
from jax.experimental import pallas as pl
from jax.experimental.pallas import tpu as pltpu
from jax.sharding import PartitionSpec as P

MAXLAG = 64
LAGS = 2 * MAXLAG
BF16, F32 = jnp.bfloat16, jnp.float32
NT = (((1,), (1,)), ((), ()))
NN = (((1,), (0,)), ((), ()))
UNROLL = 36
BAND = 16


def dot(a, b, dims=NN):
    return lax.dot_general(a, b, dims, preferred_element_type=F32)


def exact_dot(a, b):
    return lax.dot_general(a, b, NN, precision=lax.Precision.HIGHEST, preferred_element_type=F32)


def turns(first, second, period):
    product = (first * second).astype(F32)
    whole = jnp.floor((product + 0.5) * F32(0.5 / period))
    angle = (product - whole * F32(2 * period) - F32(period)) * F32(np.pi / period)
    return -jnp.cos(angle), -jnp.sin(angle)


def store_halves(ref, rows, value, times):
    width = value.shape[1]
    high = value.astype(BF16)
    low = (value - high.astype(F32)).astype(BF16)
    order = (high, low) if times == 2 else (high, high, low)
    ref[rows] = jnp.concatenate(order, 1)


def fill_tables(taps, matrix_t, table, inverse, half, group):
    length = matrix_t.shape[0]
    period = length + MAXLAG
    row = jnp.concatenate([taps[...].astype(F32), jnp.zeros((1, length - taps.shape[1]), F32)], 1)
    spread = jnp.broadcast_to(row, (length, length))
    rolled = pltpu.roll(spread, length - half, 1, stride=1, stride_axis=0).T
    distance = lax.broadcasted_iota(jnp.int32, (length, length), 1) - lax.broadcasted_iota(
        jnp.int32, (length, length), 0
    )
    matrix_t[...] = jnp.where(jnp.abs(distance) <= half, rolled, 0.0).astype(matrix_t.dtype)

    def iota(shape, dim):
        return lax.broadcasted_iota(jnp.int32, shape, dim)

    groups = period // 2 // group
    padded = groups + -groups % 8
    cos_first, sin_first = turns(2 * iota((group, length), 0) + 1, iota((group, length), 1), period)
    cos_steps, sin_steps = turns(2 * group * iota((padded, length), 0), iota((padded, length), 1), period)
    for g in range(groups):
        cos_step, sin_step = cos_steps[g : g + 1], sin_steps[g : g + 1]
        real = cos_first * cos_step - sin_first * sin_step
        imag = -(sin_first * cos_step + cos_first * sin_step)
        store_halves(table, pl.ds(2 * g * group, 2 * group), jnp.concatenate([real, imag], 0), 2)

    steps = LAGS // 8
    half_period = period // 2

    def odd(rows):
        return 2 * iota((rows, half_period), 1) + 1

    cos_first, sin_first = turns(odd(8), iota((8, half_period), 0), period)
    cos_steps, sin_steps = turns(odd(steps), 8 * iota((steps, half_period), 0) + 2 * period - MAXLAG, period)
    scale = F32(2.0 / period)
    cos_steps, sin_steps = cos_steps * scale, sin_steps * scale
    for step in range(steps):
        cos_step, sin_step = cos_steps[step : step + 1], sin_steps[step : step + 1]
        cosine = cos_first * cos_step - sin_first * sin_step
        sine = sin_first * cos_step + cos_first * sin_step
        store_halves(inverse, pl.ds(8 * step, 8), cosine, 3)
        store_halves(inverse, pl.ds(LAGS + 8 * step, 8), sine, 3)


def first_kernel(half, group, width, residues, taps, mine, mate, matrix_t, table, inverse, out):
    fill_tables(taps, matrix_t, table, inverse, half, group)
    block_kernel(width, residues, matrix_t, table, mine, mate, out)


def transform(records, matrix_t, table, width, residues):
    segs = records.shape[0] // width
    rows = [
        records[s * width + first : s * width + first + residues]
        for first in range(0, width, residues)
        for s in range(segs)
    ]
    rows = jnp.concatenate(rows, 0)
    middle = rows.shape[1] // 2
    start, stop = middle - BAND, middle + BAND
    early = dot(matrix_t[0:stop, 0:middle], rows[:, 0:middle], NT)
    late = dot(matrix_t[start:, middle:], rows[:, middle:], NT)
    filtered = jnp.concatenate(
        [early[0:start], early[start:stop] + late[0 : 2 * BAND], late[2 * BAND :]], 0
    ).astype(BF16)
    return dot(table, jnp.concatenate([filtered, filtered], 0)).astype(BF16)


def block_kernel(width, residues, matrix_t, table, *refs):
    count = len(refs) // 3
    for mine, mate, out in zip(refs[:count], refs[count : 2 * count], refs[2 * count :]):
        records = jnp.concatenate([mine[...], mate[...]], 0)
        spectra = transform(records, matrix_t[...], table[...], width, residues)
        lanes = out.shape[2]
        for index in range(out.shape[0]):
            out[index] = spectra[:, index * lanes : (index + 1) * lanes]


def bin_lanes(product, first_row, rows_per, group, rows_q):
    width = 256 // rows_q
    per = 128 // width
    lane = lax.broadcasted_iota(jnp.int32, (group, 128), 1)

    def tile(p, half):
        start = p * rows_per + first_row
        return product[start : start + group, 128 * half : 128 * half + 128]

    total = [tile(2 * per, 0), tile(per, 0) + tile(2 * per, 1), tile(0, 0) + tile(per, 1), tile(0, 1)]
    for p in range(1, per):
        kept = width * (per - p)
        moved = [
            pltpu.roll(part, kept, 1)
            for part in (tile(per + p, 0), tile(p, 0) + tile(per + p, 1), tile(p, 1))
        ]
        inside = lane < kept
        total[0] = total[0] + jnp.where(inside, 0.0, moved[0])
        total[1] = total[1] + jnp.where(inside, moved[0], moved[1])
        total[2] = total[2] + jnp.where(inside, moved[1], moved[2])
        total[3] = total[3] + jnp.where(inside, moved[2], 0.0)
    place = lax.broadcasted_iota(jnp.int32, (group, 128), 0)
    diagonal = place == (lane & (group - 1))
    return jnp.concatenate([jnp.where(diagonal, part, 0.0) for part in total], 1)


def late_kernel(
    width, residues, segs, length, src_count,
    bin_order, matrix_t, table, inverse, *refs,
):
    jitters, early, refs = refs[:2], refs[2 : src_count + 1], refs[src_count + 1 :]
    *pieces, out, spectra, edges, shifted, binned = refs
    src = lax.axis_index("src")
    owned = out.shape[0]
    rank = lax.axis_index(("src", "rcv", "seg"))
    per_line = 128 // owned
    order = pltpu.roll(bin_order[pl.ds(rank // per_line, 1), :], 128 - owned * (rank % per_line), 1)
    square = (owned, 128)
    same = lax.broadcasted_iota(jnp.int32, square, 0) == lax.broadcasted_iota(jnp.int32, square, 1)
    bins = jnp.sum(jnp.where(same, jnp.broadcast_to(order, square), 0), 1, keepdims=True)
    shift = bins[0:1, 0:1] & (residues - 1)
    per_block = width // residues
    rows_q = spectra.shape[0] - 2
    height = length + MAXLAG
    lanes = segs * residues
    step = 256 // rows_q
    group = step // 2
    last = src_count - 1
    pad = jnp.zeros((height + 16, lanes), BF16)
    spectra[0] = pad
    spectra[rows_q + 1] = pad
    one = jnp.ones((16, lanes), BF16)
    for q in range(rows_q):
        spectra[1 + q, height : height + 16] = one

    jitter = sum(ref[...] for ref in jitters)
    blocks, block_lanes = jitter.shape
    edges[...] = jnp.zeros_like(edges)
    source_lane = lax.broadcasted_iota(jnp.int32, (block_lanes, lanes), 0)
    target_lane = lax.broadcasted_iota(jnp.int32, (block_lanes, lanes), 1) & (residues - 1)
    per_row = block_lanes // residues
    for index in range(per_row):
        pick = jnp.where(source_lane == target_lane + index * residues, F32(1), F32(0))
        spread = dot(jitter.astype(BF16), pick.astype(BF16))
        for b in range(blocks):
            row = 8 + b * per_row + index
            edges[row : row + 1, :] = spread[b : b + 1, :]
    jitter_rows = edges[8 : 8 + rows_q, :]
    pairs = jnp.concatenate([edges[7:31, :], edges[8:32, :]], 1)
    pairs = jnp.concatenate([pairs, jnp.zeros((104, 2 * lanes), F32)], 0)
    jitter_columns = jnp.concatenate(
        [pairs[:, 128 * i : 128 * (i + 1)].T for i in range(2 * lanes // 128)], 0
    )

    row_lane = lax.broadcasted_iota(jnp.int32, (2 * lanes, lanes), 0)
    col_lane = lax.broadcasted_iota(jnp.int32, (2 * lanes, lanes), 1)
    bits = residues.bit_length() - 1
    same_seg = ((row_lane & (lanes - 1)) >> bits) == (col_lane >> bits)
    inside = (row_lane & (residues - 1)) - (col_lane & (residues - 1)) - shift
    place = inside + jnp.where(row_lane >= lanes, residues, 0)
    here = jnp.where(same_seg & (place == 0), F32(1), F32(0))
    after = jnp.where(same_seg & (place == 1), F32(1), F32(0))
    here_bf = here.astype(BF16)
    difference = here - after

    records = jnp.concatenate([piece[...] for piece in pieces], 0)
    fresh = transform(records, matrix_t[...], table[...], width, residues)
    for index in range(per_block):
        spectra[1 + per_block * (src ^ last) + index, 0:height] = fresh[:, index * lanes : (index + 1) * lanes]
    for k in range(last):
        for index in range(per_block):
            spectra[1 + per_block * (src ^ k) + index, 0:height] = early[k][index]

    for p in range(rows_q + 1):
        mix = after + difference * jitter_columns[:, p : p + 1]
        mapping = jnp.concatenate([here_bf, mix.astype(BF16)], 1)
        both = jnp.concatenate([spectra[p], spectra[p + 1]], 1)
        shifted[p] = dot(both, mapping).astype(BF16)

    upper = jitter_rows.astype(BF16)
    lower = (1.0 - jitter_rows).astype(BF16)

    swap = (lax.broadcasted_iota(jnp.int32, (height // 2, 128), 1) & group) == 0

    def cross(imag):
        tiles = [imag[:, 128 * i : 128 * (i + 1)] for i in range(4)]
        return jnp.concatenate(
            [jnp.where(swap, pltpu.roll(tile, 128 - group, 1), -pltpu.roll(tile, group, 1)) for tile in tiles], 1
        )

    def one_group(g, carry):
        rows = pl.ds(pl.multiple_of(g * step, step), step)
        left = []
        for q in range(rows_q):
            values = spectra[1 + q, rows]
            left.append(jnp.concatenate([values * lower[q : q + 1], values * upper[q : q + 1]], 1))
        right = [shifted[p, rows] for p in range(rows_q + 1)]
        product = dot(jnp.concatenate(right, 0), jnp.concatenate(left, 0), NT)
        for part in range(2):
            place = pl.ds(pl.multiple_of(g * group, group), group)
            binned[part, place] = bin_lanes(product, part * group, step, group, rows_q)
        return carry

    lax.fori_loop(0, height // step, one_group, 0, unroll=UNROLL)

    count_left = []
    for q in range(rows_q):
        row = jnp.concatenate([lower[q : q + 1], upper[q : q + 1]], 1)
        count_left.append(jnp.broadcast_to(row, (step, 2 * lanes)))
    ones_rows = [shifted[p, height : height + 16] for p in range(rows_q + 1)]
    counted = dot(jnp.concatenate(ones_rows, 0), jnp.concatenate(count_left, 0), NT)
    if group > 8:
        counted = jnp.concatenate([counted[16 * p : 16 * p + 16] for p in range(rows_q + 1)], 0)
    counts = jnp.sum(bin_lanes(counted, 0, 16, group, rows_q), 0, keepdims=True)

    values = binned[0] + cross(binned[1])
    high = values.astype(BF16)
    low = (values - high.astype(F32)).astype(BF16)
    lagged = dot(inverse[...], jnp.concatenate([high, low, high], 0))
    lane = lax.broadcasted_iota(jnp.int32, (LAGS, 512), 1)
    lagged = jnp.where((lane & group) == 0, lagged[0:LAGS], lagged[LAGS:])
    high = lagged.astype(BF16)
    low = (lagged - high.astype(F32)).astype(BF16)

    lane = lax.broadcasted_iota(jnp.int32, (owned, 512), 1)
    lane_bin = 2 * rows_q - 1 - (lane >> (step.bit_length() - 1))
    picked = (bins >> (residues.bit_length() - 1)) == lane_bin
    weights = jnp.where(picked, F32(1), F32(0))
    total = dot(
        jnp.concatenate([weights, weights], 1).astype(BF16), jnp.concatenate([high, low], 1), NT
    )
    count = jnp.sum(jnp.where((lane & (step - 1)) == 0, weights * counts, 0.0), 1, keepdims=True) / segs
    out[...] = total * lax.rsqrt(jnp.maximum(count, 1.0) * (segs * length))


def cost(microseconds):
    return pl.CostEstimate(
        flops=int(microseconds * 1e9), bytes_accessed=int(microseconds * 3e6), transcendentals=0
    )


def partners(axis, step):
    return [(index, index ^ step) for index in range(lax.axis_size(axis))]


def on_device(traces, fir_taps, pair_bins, bin_order):
    seg_local, width, length = traces.shape
    src_count, rcv_count, seg_count = (lax.axis_size(axis) for axis in ("src", "rcv", "seg"))
    segs = seg_local * seg_count
    channels = width * src_count
    owners = src_count * rcv_count * seg_count
    residues = owners
    rows_q = channels // residues
    lanes = segs * residues
    period = length + MAXLAG
    owned = bin_order.shape[0] // owners

    mine = traces.reshape(seg_local * width, length)
    def to_mate(piece):
        return lax.ppermute(piece, "seg", partners("seg", 1))

    received = [mine] + [lax.ppermute(mine, "src", partners("src", k)) for k in range(1, src_count)]
    mates = [to_mate(mine)]

    src, rcv = lax.axis_index("src"), lax.axis_index("rcv")
    assert src_count == rcv_count and fir_taps.shape[0] // 2 <= BAND
    channel = jnp.arange(width, dtype=jnp.int32)[None, :]
    of_receivers = pair_bins[width - 1 : width, :] - (rcv * width + channel)
    of_sources = channels - (src * width + channel) - pair_bins[:, 0:1].reshape(1, width)
    slots = jnp.arange(rcv_count, dtype=jnp.int32)[:, None]
    jitter = jnp.where((slots == rcv) & (src == src_count - 1), of_receivers, 0)
    jitter = (jitter + jnp.where((slots == src) & (rcv == 0), of_sources, 0)).astype(F32)

    vmem = pl.BlockSpec(memory_space=pltpu.VMEM)
    last = src_count - 1
    per_block = width // residues
    params = pltpu.CompilerParams(vmem_limit_bytes=(20 if lanes <= 128 else 40) * 2**20)
    group = 128 // rows_q
    matrix_t, table, inverse, first = pl.pallas_call(
        functools.partial(first_kernel, fir_taps.shape[0] // 2, group, width, residues),
        out_shape=[
            jax.ShapeDtypeStruct((length, length), BF16),
            jax.ShapeDtypeStruct((period, 2 * length), BF16),
            jax.ShapeDtypeStruct((2 * LAGS, 3 * period // 2), BF16),
            jax.ShapeDtypeStruct((per_block, period, lanes), BF16),
        ],
        in_specs=[vmem] * 3,
        out_specs=[vmem] * 4,
        compiler_params=params,
        cost_estimate=cost(0.01),
        name="tables_and_own_spectra",
    )(fir_taps[None, :], mine, mates[0])

    def block_spectra(blocks):
        return pl.pallas_call(
            functools.partial(block_kernel, width, residues),
            out_shape=[jax.ShapeDtypeStruct((per_block, period, lanes), BF16) for _ in blocks],
            in_specs=[vmem] * (2 + 2 * len(blocks)),
            out_specs=[vmem] * len(blocks),
            compiler_params=params,
            cost_estimate=cost(0.01),
            name="block_spectra",
        )(matrix_t, table, *[received[k] for k in blocks], *[mates[k] for k in blocks])

    bits = [1 << bit for bit in range(1, (src_count - 1).bit_length())]
    hops = [(0, bit) for bit in bits] + [(1, 1)] + [(bit, 0) for bit in bits]
    arrived = jnp.zeros_like(jitter)
    for turn, (over_src, over_rcv) in enumerate(hops):
        if turn == len(hops) - 2:
            arrived, first = lax.optimization_barrier((arrived, first))
        if turn == len(hops) - 1:
            *received[1:], first, arrived = lax.optimization_barrier((*received[1:], first, arrived))
        jitter = jitter + arrived
        pairs = [
            (i * rcv_count + z, (i ^ over_src) * rcv_count + (z ^ over_rcv))
            for i in range(src_count)
            for z in range(rcv_count)
        ]
        arrived = lax.ppermute(jitter, ("src", "rcv"), pairs)
    jitters = [jitter, arrived]
    mates += [to_mate(block) for block in received[1:]]
    early = [first, *block_spectra(range(1, last))]
    return pl.pallas_call(
        functools.partial(late_kernel, width, residues, segs, length, src_count),
        out_shape=jax.ShapeDtypeStruct((owned, LAGS), F32),
        in_specs=[vmem] * (last + 8),
        out_specs=vmem,
        scratch_shapes=[
            pltpu.VMEM((rows_q + 2, period + 16, lanes), BF16),
            pltpu.VMEM((32, lanes), F32),
            pltpu.VMEM((rows_q + 1, period + 16, 2 * lanes), BF16),
            pltpu.VMEM((2, period // 2, 512), F32),
        ],
        compiler_params=params,
        cost_estimate=cost(0.01),
        name="bin_stacks",
    )(bin_order.reshape(-1, 128), matrix_t, table, inverse, *jitters, *early, received[last], mates[last])


def solution(mesh):
    return jax.shard_map(
        on_device,
        mesh=mesh,
        in_specs=(P("seg", "src", None), P(), P("src", "rcv"), P()),
        out_specs=P(("src", "rcv", "seg"), None),
        check_vma=False,
    )
```

```python
import functools

import jax
import jax.numpy as jnp
import numpy as np
from jax import lax
from jax.experimental import pallas as pl
from jax.experimental.pallas import tpu as pltpu
from jax.sharding import PartitionSpec as P

MAXLAG = 64
LAGS = 2 * MAXLAG
BF16, F32 = jnp.bfloat16, jnp.float32
NT = (((1,), (1,)), ((), ()))
NN = (((1,), (0,)), ((), ()))
UNROLL = 36
BAND = 16


def dot(a, b, dims=NN):
    return lax.dot_general(a, b, dims, preferred_element_type=F32)


def exact_dot(a, b):
    return lax.dot_general(a, b, NN, precision=lax.Precision.HIGHEST, preferred_element_type=F32)


def turns(first, second, period):
    product = (first * second).astype(F32)
    whole = jnp.floor((product + 0.5) * F32(0.5 / period))
    angle = (product - whole * F32(2 * period) - F32(period)) * F32(np.pi / period)
    return -jnp.cos(angle), -jnp.sin(angle)


def store_halves(ref, rows, value, times):
    width = value.shape[1]
    high = value.astype(BF16)
    low = (value - high.astype(F32)).astype(BF16)
    order = (high, low) if times == 2 else (high, high, low)
    ref[rows] = jnp.concatenate(order, 1)


def fill_tables(taps, matrix_t, table, inverse, half, group):
    length = matrix_t.shape[0]
    period = length + MAXLAG
    row = jnp.concatenate([taps[...].astype(F32), jnp.zeros((1, length - taps.shape[1]), F32)], 1)
    spread = jnp.broadcast_to(row, (length, length))
    rolled = pltpu.roll(spread, length - half, 1, stride=1, stride_axis=0).T
    distance = lax.broadcasted_iota(jnp.int32, (length, length), 1) - lax.broadcasted_iota(
        jnp.int32, (length, length), 0
    )
    matrix_t[...] = jnp.where(jnp.abs(distance) <= half, rolled, 0.0).astype(matrix_t.dtype)

    def iota(shape, dim):
        return lax.broadcasted_iota(jnp.int32, shape, dim)

    groups = period // 2 // group
    padded = groups + -groups % 8
    cos_first, sin_first = turns(2 * iota((group, length), 0) + 1, iota((group, length), 1), period)
    cos_steps, sin_steps = turns(2 * group * iota((padded, length), 0), iota((padded, length), 1), period)
    for g in range(groups):
        cos_step, sin_step = cos_steps[g : g + 1], sin_steps[g : g + 1]
        real = cos_first * cos_step - sin_first * sin_step
        imag = -(sin_first * cos_step + cos_first * sin_step)
        store_halves(table, pl.ds(2 * g * group, 2 * group), jnp.concatenate([real, imag], 0), 2)

    steps = LAGS // 8
    half_period = period // 2

    def odd(rows):
        return 2 * iota((rows, half_period), 1) + 1

    cos_first, sin_first = turns(odd(8), iota((8, half_period), 0), period)
    cos_steps, sin_steps = turns(odd(steps), 8 * iota((steps, half_period), 0) + 2 * period - MAXLAG, period)
    scale = F32(2.0 / period)
    cos_steps, sin_steps = cos_steps * scale, sin_steps * scale
    for step in range(steps):
        cos_step, sin_step = cos_steps[step : step + 1], sin_steps[step : step + 1]
        cosine = cos_first * cos_step - sin_first * sin_step
        sine = sin_first * cos_step + cos_first * sin_step
        store_halves(inverse, pl.ds(8 * step, 8), cosine, 3)
        store_halves(inverse, pl.ds(LAGS + 8 * step, 8), sine, 3)


def first_kernel(half, group, width, residues, taps, mine, mate, matrix_t, table, inverse, out):
    fill_tables(taps, matrix_t, table, inverse, half, group)
    block_kernel(width, residues, matrix_t, table, mine, mate, out)


def transform(records, matrix_t, table, width, residues):
    segs = records.shape[0] // width
    rows = [
        records[s * width + first : s * width + first + residues]
        for first in range(0, width, residues)
        for s in range(segs)
    ]
    rows = jnp.concatenate(rows, 0)
    middle = rows.shape[1] // 2
    start, stop = middle - BAND, middle + BAND
    early = dot(matrix_t[0:stop, 0:middle], rows[:, 0:middle], NT)
    late = dot(matrix_t[start:, middle:], rows[:, middle:], NT)
    filtered = jnp.concatenate(
        [early[0:start], early[start:stop] + late[0 : 2 * BAND], late[2 * BAND :]], 0
    ).astype(BF16)
    length, height = filtered.shape[0], table.shape[0]
    halves = dot(jnp.concatenate([table[:, 0:length], table[:, length:]], 0), filtered)
    return (halves[0:height] + halves[height:]).astype(BF16)


def block_kernel(width, residues, matrix_t, table, *refs):
    count = len(refs) // 3
    for mine, mate, out in zip(refs[:count], refs[count : 2 * count], refs[2 * count :]):
        records = jnp.concatenate([mine[...], mate[...]], 0)
        spectra = transform(records, matrix_t[...], table[...], width, residues)
        lanes = out.shape[2]
        for index in range(out.shape[0]):
            out[index] = spectra[:, index * lanes : (index + 1) * lanes]


def bin_lanes(product, first_row, rows_per, group, rows_q):
    width = 256 // rows_q
    per = 128 // width
    lane = lax.broadcasted_iota(jnp.int32, (group, 128), 1)

    def tile(p, half):
        start = p * rows_per + first_row
        return product[start : start + group, 128 * half : 128 * half + 128]

    total = [tile(2 * per, 0), tile(per, 0) + tile(2 * per, 1), tile(0, 0) + tile(per, 1), tile(0, 1)]
    for p in range(1, per):
        kept = width * (per - p)
        moved = [
            pltpu.roll(part, kept, 1)
            for part in (tile(per + p, 0), tile(p, 0) + tile(per + p, 1), tile(p, 1))
        ]
        inside = lane < kept
        total[0] = total[0] + jnp.where(inside, 0.0, moved[0])
        total[1] = total[1] + jnp.where(inside, moved[0], moved[1])
        total[2] = total[2] + jnp.where(inside, moved[1], moved[2])
        total[3] = total[3] + jnp.where(inside, moved[2], 0.0)
    place = lax.broadcasted_iota(jnp.int32, (group, 128), 0)
    diagonal = place == (lane & (group - 1))
    return jnp.concatenate([jnp.where(diagonal, part, 0.0) for part in total], 1)


def late_kernel(
    width, residues, segs, length, src_count,
    bin_order, matrix_t, table, inverse, *refs,
):
    jitters, early, refs = refs[:2], refs[2 : src_count + 1], refs[src_count + 1 :]
    *pieces, out, spectra, edges, shifted, binned = refs
    src = lax.axis_index("src")
    owned = out.shape[0]
    rank = lax.axis_index(("src", "rcv", "seg"))
    per_line = 128 // owned
    order = pltpu.roll(bin_order[pl.ds(rank // per_line, 1), :], 128 - owned * (rank % per_line), 1)
    square = (owned, 128)
    same = lax.broadcasted_iota(jnp.int32, square, 0) == lax.broadcasted_iota(jnp.int32, square, 1)
    bins = jnp.sum(jnp.where(same, jnp.broadcast_to(order, square), 0), 1, keepdims=True)
    shift = bins[0:1, 0:1] & (residues - 1)
    per_block = width // residues
    rows_q = spectra.shape[0] - 2
    height = length + MAXLAG
    lanes = segs * residues
    step = 256 // rows_q
    group = step // 2
    last = src_count - 1
    pad = jnp.zeros((height + 16, lanes), BF16)
    spectra[0] = pad
    spectra[rows_q + 1] = pad
    one = jnp.ones((16, lanes), BF16)
    for q in range(rows_q):
        spectra[1 + q, height : height + 16] = one

    jitter = sum(ref[...] for ref in jitters)
    blocks, block_lanes = jitter.shape
    edges[...] = jnp.zeros_like(edges)
    source_lane = lax.broadcasted_iota(jnp.int32, (block_lanes, lanes), 0)
    target_lane = lax.broadcasted_iota(jnp.int32, (block_lanes, lanes), 1) & (residues - 1)
    per_row = block_lanes // residues
    for index in range(per_row):
        pick = jnp.where(source_lane == target_lane + index * residues, F32(1), F32(0))
        spread = dot(jitter.astype(BF16), pick.astype(BF16))
        for b in range(blocks):
            row = 8 + b * per_row + index
            edges[row : row + 1, :] = spread[b : b + 1, :]
    jitter_rows = edges[8 : 8 + rows_q, :]
    pairs = jnp.concatenate([edges[7:31, :], edges[8:32, :]], 1)
    pairs = jnp.concatenate([pairs, jnp.zeros((104, 2 * lanes), F32)], 0)
    jitter_columns = jnp.concatenate(
        [pairs[:, 128 * i : 128 * (i + 1)].T for i in range(2 * lanes // 128)], 0
    )

    row_lane = lax.broadcasted_iota(jnp.int32, (2 * lanes, lanes), 0)
    col_lane = lax.broadcasted_iota(jnp.int32, (2 * lanes, lanes), 1)
    bits = residues.bit_length() - 1
    same_seg = ((row_lane & (lanes - 1)) >> bits) == (col_lane >> bits)
    inside = (row_lane & (residues - 1)) - (col_lane & (residues - 1)) - shift
    place = inside + jnp.where(row_lane >= lanes, residues, 0)
    here = jnp.where(same_seg & (place == 0), F32(1), F32(0))
    after = jnp.where(same_seg & (place == 1), F32(1), F32(0))
    here_bf = here.astype(BF16)
    difference = here - after

    records = jnp.concatenate([piece[...] for piece in pieces], 0)
    fresh = transform(records, matrix_t[...], table[...], width, residues)
    for index in range(per_block):
        spectra[1 + per_block * (src ^ last) + index, 0:height] = fresh[:, index * lanes : (index + 1) * lanes]
    for k in range(last):
        for index in range(per_block):
            spectra[1 + per_block * (src ^ k) + index, 0:height] = early[k][index]

    for p in range(rows_q + 1):
        mix = after + difference * jitter_columns[:, p : p + 1]
        mapping = jnp.concatenate([here_bf, mix.astype(BF16)], 1)
        both = jnp.concatenate([spectra[p], spectra[p + 1]], 1)
        shifted[p] = dot(both, mapping).astype(BF16)

    upper = jitter_rows.astype(BF16)
    lower = (1.0 - jitter_rows).astype(BF16)

    swap = (lax.broadcasted_iota(jnp.int32, (height // 2, 128), 1) & group) == 0

    def cross(imag):
        tiles = [imag[:, 128 * i : 128 * (i + 1)] for i in range(4)]
        return jnp.concatenate(
            [jnp.where(swap, pltpu.roll(tile, 128 - group, 1), -pltpu.roll(tile, group, 1)) for tile in tiles], 1
        )

    def one_group(g, carry):
        rows = pl.ds(pl.multiple_of(g * step, step), step)
        left = []
        for q in range(rows_q):
            values = spectra[1 + q, rows]
            left.append(jnp.concatenate([values * lower[q : q + 1], values * upper[q : q + 1]], 1))
        right = [shifted[p, rows] for p in range(rows_q + 1)]
        product = dot(jnp.concatenate(right, 0), jnp.concatenate(left, 0), NT)
        for part in range(2):
            place = pl.ds(pl.multiple_of(g * group, group), group)
            binned[part, place] = bin_lanes(product, part * group, step, group, rows_q)
        return carry

    lax.fori_loop(0, height // step, one_group, 0, unroll=UNROLL)

    count_left = []
    for q in range(rows_q):
        row = jnp.concatenate([lower[q : q + 1], upper[q : q + 1]], 1)
        count_left.append(jnp.broadcast_to(row, (step, 2 * lanes)))
    ones_rows = [shifted[p, height : height + 16] for p in range(rows_q + 1)]
    counted = dot(jnp.concatenate(ones_rows, 0), jnp.concatenate(count_left, 0), NT)
    if group > 8:
        counted = jnp.concatenate([counted[16 * p : 16 * p + 16] for p in range(rows_q + 1)], 0)
    counts = jnp.sum(bin_lanes(counted, 0, 16, group, rows_q), 0, keepdims=True)

    values = binned[0] + cross(binned[1])
    high = values.astype(BF16)
    low = (values - high.astype(F32)).astype(BF16)
    lagged = dot(inverse[...], jnp.concatenate([high, low, high], 0))
    lane = lax.broadcasted_iota(jnp.int32, (LAGS, 512), 1)
    lagged = jnp.where((lane & group) == 0, lagged[0:LAGS], lagged[LAGS:])
    high = lagged.astype(BF16)
    low = (lagged - high.astype(F32)).astype(BF16)

    lane = lax.broadcasted_iota(jnp.int32, (owned, 512), 1)
    lane_bin = 2 * rows_q - 1 - (lane >> (step.bit_length() - 1))
    picked = (bins >> (residues.bit_length() - 1)) == lane_bin
    weights = jnp.where(picked, F32(1), F32(0))
    total = dot(
        jnp.concatenate([weights, weights], 1).astype(BF16), jnp.concatenate([high, low], 1), NT
    )
    count = jnp.sum(jnp.where((lane & (step - 1)) == 0, weights * counts, 0.0), 1, keepdims=True) / segs
    out[...] = total * lax.rsqrt(jnp.maximum(count, 1.0) * (segs * length))


def cost(microseconds):
    return pl.CostEstimate(
        flops=int(microseconds * 1e9), bytes_accessed=int(microseconds * 3e6), transcendentals=0
    )


def partners(axis, step):
    return [(index, index ^ step) for index in range(lax.axis_size(axis))]


def on_device(traces, fir_taps, pair_bins, bin_order):
    seg_local, width, length = traces.shape
    src_count, rcv_count, seg_count = (lax.axis_size(axis) for axis in ("src", "rcv", "seg"))
    segs = seg_local * seg_count
    channels = width * src_count
    owners = src_count * rcv_count * seg_count
    residues = owners
    rows_q = channels // residues
    lanes = segs * residues
    period = length + MAXLAG
    owned = bin_order.shape[0] // owners

    mine = traces.reshape(seg_local * width, length)
    def to_mate(piece):
        return lax.ppermute(piece, "seg", partners("seg", 1))

    received = [mine] + [lax.ppermute(mine, "src", partners("src", k)) for k in range(1, src_count)]
    mates = [to_mate(mine)]

    src, rcv = lax.axis_index("src"), lax.axis_index("rcv")
    assert src_count == rcv_count and fir_taps.shape[0] // 2 <= BAND
    channel = jnp.arange(width, dtype=jnp.int32)[None, :]
    of_receivers = pair_bins[width - 1 : width, :] - (rcv * width + channel)
    of_sources = channels - (src * width + channel) - pair_bins[:, 0:1].reshape(1, width)
    slots = jnp.arange(rcv_count, dtype=jnp.int32)[:, None]
    jitter = jnp.where((slots == rcv) & (src == src_count - 1), of_receivers, 0)
    jitter = (jitter + jnp.where((slots == src) & (rcv == 0), of_sources, 0)).astype(F32)

    vmem = pl.BlockSpec(memory_space=pltpu.VMEM)
    last = src_count - 1
    per_block = width // residues
    params = pltpu.CompilerParams(vmem_limit_bytes=(20 if lanes <= 128 else 40) * 2**20)
    group = 128 // rows_q
    matrix_t, table, inverse, first = pl.pallas_call(
        functools.partial(first_kernel, fir_taps.shape[0] // 2, group, width, residues),
        out_shape=[
            jax.ShapeDtypeStruct((length, length), BF16),
            jax.ShapeDtypeStruct((period, 2 * length), BF16),
            jax.ShapeDtypeStruct((2 * LAGS, 3 * period // 2), BF16),
            jax.ShapeDtypeStruct((per_block, period, lanes), BF16),
        ],
        in_specs=[vmem] * 3,
        out_specs=[vmem] * 4,
        compiler_params=params,
        cost_estimate=cost(0.01),
        name="tables_and_own_spectra",
    )(fir_taps[None, :], mine, mates[0])

    def block_spectra(blocks):
        return pl.pallas_call(
            functools.partial(block_kernel, width, residues),
            out_shape=[jax.ShapeDtypeStruct((per_block, period, lanes), BF16) for _ in blocks],
            in_specs=[vmem] * (2 + 2 * len(blocks)),
            out_specs=[vmem] * len(blocks),
            compiler_params=params,
            cost_estimate=cost(0.01),
            name="block_spectra",
        )(matrix_t, table, *[received[k] for k in blocks], *[mates[k] for k in blocks])

    bits = [1 << bit for bit in range(1, (src_count - 1).bit_length())]
    hops = [(0, bit) for bit in bits] + [(1, 1)] + [(bit, 0) for bit in bits]
    arrived = jnp.zeros_like(jitter)
    for turn, (over_src, over_rcv) in enumerate(hops):
        if turn == len(hops) - 2:
            arrived, first = lax.optimization_barrier((arrived, first))
        if turn == len(hops) - 1:
            *received[1:], first, arrived = lax.optimization_barrier((*received[1:], first, arrived))
        jitter = jitter + arrived
        pairs = [
            (i * rcv_count + z, (i ^ over_src) * rcv_count + (z ^ over_rcv))
            for i in range(src_count)
            for z in range(rcv_count)
        ]
        arrived = lax.ppermute(jitter, ("src", "rcv"), pairs)
    jitters = [jitter, arrived]
    mates += [to_mate(block) for block in received[1:]]
    early = [first, *block_spectra(range(1, last))]
    return pl.pallas_call(
        functools.partial(late_kernel, width, residues, segs, length, src_count),
        out_shape=jax.ShapeDtypeStruct((owned, LAGS), F32),
        in_specs=[vmem] * (last + 8),
        out_specs=vmem,
        scratch_shapes=[
            pltpu.VMEM((rows_q + 2, period + 16, lanes), BF16),
            pltpu.VMEM((32, lanes), F32),
            pltpu.VMEM((rows_q + 1, period + 16, 2 * lanes), BF16),
            pltpu.VMEM((2, period // 2, 512), F32),
        ],
        compiler_params=params,
        cost_estimate=cost(0.01),
        name="bin_stacks",
    )(bin_order.reshape(-1, 128), matrix_t, table, inverse, *jitters, *early, received[last], mates[last])


def solution(mesh):
    return jax.shard_map(
        on_device,
        mesh=mesh,
        in_specs=(P("seg", "src", None), P(), P("src", "rcv"), P()),
        out_specs=P(("src", "rcv", "seg"), None),
        check_vma=False,
    )
```
